128 devices in a mesh: row: 16 (over z_hi, y, core), col: 8 (over x, z_lo).
Axes of the slice: x: 4, y: 4, z: 4 (z_hi: 2, z_lo: 2; z = z_hi * 2 + z_lo), core: 2. Of those that a mesh axis runs over, the one named last changes fastest.
Arguments:
- operator: bfloat16 [36864, 36864], P('row', 'col'), may hold values from -0.046875 to 0.046875
- sketch_right: bfloat16 [36864, 384], P(('col', 'row')), may hold values from -6 to 6
- sketch_left: bfloat16 [36864, 576], P(('row', 'col')), may hold values from -6 to 6
Outputs:
- left_factor: bfloat16 [36864, 384], P('row')
- right_factor: bfloat16 [36864, 384], P(('col', 'row'))
The draws below stay inside these ranges and needn't reach their ends.
All inputs are finite; a program needn't handle non-finite values.
Results may differ from the reference program's by a relative error of at most 0.0015.
Values may be sent and summed in bfloat16 or wider, within the bound.
No kernel may reach another device: no remote copies, remote signals or barrier semaphores. Data moves between devices by JAX's collectives and lax.ppermute only.
A program may use at most 128 MiB of HBM per device.

```python
import math
import jax
import jax.numpy as jnp
from jax import lax

N = 36864
R = 384
L = 576


def raised(entries, rng, source, target, shards_of, factor):
    owner, partner = [(jnp.arange(entries.shape[position]) // (entries.shape[position] // shards_of)).reshape([-1 if axis == position else 1 for axis in range(entries.ndim)]) for position in (source, target)]
    chosen = jax.random.permutation(rng, shards_of)[partner]
    strong = (owner == chosen) | (owner == (partner + shards_of // 2) % shards_of)
    return jnp.where(strong, factor * entries, entries)


def level_of(key, dims, shards, least, high):
    factor_of, own = 1.0, jax.random.fold_in(key, 6)
    for dim, parts in shards:
        heights = jnp.exp(jax.random.uniform(jax.random.fold_in(own, dim), (parts,), jnp.float32, least / len(shards), high / len(shards)))
        factor_of = factor_of * jnp.repeat(heights, dims[dim] // parts).reshape([-1 if axis == dim else 1 for axis in range(len(dims))])
    return factor_of


def gaussian(stream_key, dims, deviation, most, shards=(), kind=jnp.bfloat16):
    array = deviation * jax.random.normal(stream_key, dims, jnp.float32)
    if shards:
        array = array * level_of(stream_key, dims, shards, -0.22, 0.18)
    return jnp.clip(array, -most, most).astype(kind)


def heavy_noise(key, dims, spread, most, split, heavy, kind=jnp.bfloat16):
    drawn = spread * jax.random.normal(key, dims, jnp.float32)
    if split:
        drawn = drawn * level_of(key, dims, split, -0.22, 0.18)
    return jnp.clip(raised(drawn, jax.random.fold_in(key, 3), *heavy), -most, most).astype(kind)


def setup_inputs(seed: int = 0) -> dict:
    key_of = jax.random.split(jax.random.key(seed), 4)
    operator = heavy_noise(key_of[0], (N, N), N ** -0.5, 0.046875, ((0, 16), (1, 8)), (0, 1, 16, 2.0))
    sketch_right = gaussian(key_of[1], (N, R), 1.0, 6.0, ((0, 128),))
    sketch_left = gaussian(key_of[2], (N, L), 1.0, 6.0, ((0, 128),))
    return dict(operator=operator, sketch_right=sketch_right, sketch_left=sketch_left)


def transposed_product(wide, sketch):
    contract = (((0,), (0,)), ((), ()))
    high_part = wide.astype(jnp.bfloat16)
    rest = wide - lax.optimization_barrier(high_part).astype(jnp.float32)
    middle_part = rest.astype(jnp.bfloat16)
    low_part = (rest - lax.optimization_barrier(middle_part).astype(jnp.float32)).astype(jnp.bfloat16)
    total = lax.dot_general(high_part.astype(jnp.float32), sketch.astype(jnp.float32), contract, preferred_element_type=jnp.float32)
    total = total + lax.dot_general(middle_part.astype(jnp.float32), sketch.astype(jnp.float32), contract, preferred_element_type=jnp.float32)
    return total + lax.dot_general(low_part.astype(jnp.float32), sketch.astype(jnp.float32), contract, preferred_element_type=jnp.float32)

def reference(operator, sketch_right, sketch_left):
    image = jnp.dot(operator.astype(jnp.float32), sketch_right.astype(jnp.float32), preferred_element_type=jnp.float32)
    wide = lax.dot_general(operator.astype(jnp.float32), sketch_left.astype(jnp.float32), (((0,), (0,)), ((), ())), preferred_element_type=jnp.float32)
    core = transposed_product(wide, sketch_right)
    gram = jnp.dot(core.T, core, precision=lax.Precision.HIGHEST)
    lower = jnp.linalg.cholesky(gram)
    identity = jnp.eye(gram.shape[0], dtype=jnp.float32)
    inverse = jax.scipy.linalg.solve_triangular(lower, identity, lower=True).T
    ortho = jnp.dot(core, inverse, precision=lax.Precision.HIGHEST)
    factor = math.sqrt(N * L)
    left_factor = (factor * jnp.dot(image, inverse, precision=lax.Precision.HIGHEST)).astype(jnp.bfloat16)
    right_factor = jnp.dot(wide, ortho, precision=lax.Precision.HIGHEST).astype(jnp.bfloat16)
    return (left_factor, right_factor)
```

```python
import functools
import math

import jax
import jax.numpy as jnp
from jax import lax
from jax.experimental import pallas as pl
from jax.experimental.pallas import tpu as pltpu
from jax.sharding import PartitionSpec as P

N = 36864
L = 576
BLOCK = 128
PANEL = 16
HIGHEST = lax.Precision.HIGHEST
TRANSPOSED = (((0,), (0,)), ((), ()))
CORE, ROW_RING, ROW_Z = 1, (2, 6, 4), 8
COL_RING, COL_Z = (2, 6, 4), 1


def three_parts(value):
    high_part = value.astype(jnp.bfloat16)
    rest = value - lax.optimization_barrier(high_part).astype(jnp.float32)
    middle_part = rest.astype(jnp.bfloat16)
    low_part = (rest - lax.optimization_barrier(middle_part).astype(jnp.float32)).astype(
        jnp.bfloat16
    )
    return high_part, middle_part, low_part


def kernel_parts(value):
    high = value.astype(jnp.bfloat16).astype(jnp.float32)
    rest = value - high
    middle = rest.astype(jnp.bfloat16).astype(jnp.float32)
    low = (rest - middle).astype(jnp.bfloat16).astype(jnp.float32)
    return high, middle, low


def rank_update(value):
    high, middle, low = kernel_parts(value)
    left = jnp.concatenate([high, high, middle, high, low, middle], 0).astype(jnp.bfloat16)
    right = jnp.concatenate([high, middle, high, low, high, middle], 0).astype(jnp.bfloat16)
    return lax.dot_general(left, right, TRANSPOSED, preferred_element_type=jnp.float32)


def block_factor(block_ref):
    size = block_ref.shape[0]
    row = lax.broadcasted_iota(jnp.int32, (PANEL, size), 0)
    lane = lax.broadcasted_iota(jnp.int32, (PANEL, size), 1)
    for start in range(0, size, PANEL):
        end = start + PANEL
        panel = block_ref[start:end, :]
        rows = jnp.where(
            (lane >= start) & (lane < end), (lane - start == row).astype(jnp.float32), panel
        )
        columns = [
            jnp.broadcast_to(panel[:, start + j : start + j + 1], (PANEL, size))
            for j in range(PANEL)
        ]
        pivots = jnp.ones((PANEL, size), jnp.float32)
        for i in range(PANEL):
            pivot = columns[i][i : i + 1, :]
            multiple = jnp.where(row > i, columns[i] * (1.0 / pivot), 0.0)
            pivots = jnp.where(row == i, pivot, pivots)
            for j in range(i + 1, PANEL):
                columns[j] = columns[j] - multiple * columns[j][i : i + 1, :]
            rows = rows - multiple * rows[i : i + 1, :]
        rows = rows * lax.rsqrt(pivots)
        block_ref[start:end, :] = rows
        if end < size:
            below = lax.broadcasted_iota(jnp.int32, (size - end, size), 1)
            rest = jnp.where((below >= start) & (below < end), 0.0, block_ref[end:, :])
            block_ref[end:, :] = rest - rank_update(rows)[end:, :]
    down = lax.broadcasted_iota(jnp.int32, (size, size), 0)
    across = lax.broadcasted_iota(jnp.int32, (size, size), 1)
    return jnp.where(down >= across, block_ref[...], 0.0)


def factor_kernel(core_ref, lower_inverse_ref, ortho_ref, block_ref):
    core = core_ref[...]
    size = core.shape[1]
    work = lower_inverse_ref
    dot = functools.partial(
        lax.dot_general, precision=HIGHEST, preferred_element_type=jnp.float32
    )
    work[...] = dot(core, core, TRANSPOSED)
    starts = range(0, size, BLOCK)
    for low in starts:
        high = low + BLOCK
        block_ref[...] = work[low:high, low:high]
        inverse = block_factor(block_ref)
        strip = dot(inverse, work[low:high, :], (((1,), (0,)), ((), ())))
        strip = jnp.concatenate(
            [inverse if at == low else strip[:, at : at + BLOCK] for at in starts], 1
        )
        if high < size:
            change = dot(strip[:, high:], strip, TRANSPOSED)
            for at in starts:
                old = 0.0 if at == low else work[high:, at : at + BLOCK]
                work[high:, at : at + BLOCK] = old - change[:, at : at + BLOCK]
        for at in starts:
            kept = strip[:, at : at + BLOCK]
            work[low:high, at : at + BLOCK] = kept if at <= low else jnp.zeros_like(kept)
    ortho_ref[...] = dot(core, work[...], (((1,), (1,)), ((), ())))


def factors_of(core):
    tall, size = core.shape
    return pl.pallas_call(
        factor_kernel,
        out_shape=[
            jax.ShapeDtypeStruct((size, size), jnp.float32),
            jax.ShapeDtypeStruct((tall, size), jnp.float32),
        ],
        scratch_shapes=[pltpu.VMEM((BLOCK, BLOCK), jnp.float32)],
        compiler_params=pltpu.CompilerParams(vmem_limit_bytes=32 * 2**20),
        cost_estimate=pl.CostEstimate(
            flops=20 * 10**9, bytes_accessed=3 * 10**6, transcendentals=0
        ),
    )(core)


def swap(value, axis, count, mask):
    return lax.ppermute(value, axis, [(i, i ^ mask) for i in range(count)])


def gather_direct(value, axes, count):
    copies = jnp.broadcast_to(value[None], (count,) + value.shape)
    return lax.all_to_all(copies, axes, 0, 0)


def sum_everywhere(value, count):
    pieces = value.reshape(count, -1)
    share = lax.all_to_all(pieces, ("row", "col"), 0, 0).sum(0)
    return gather_direct(share, ("row", "col"), count).reshape(value.shape)


def gather_grid(value, axis, count, ring, across, shift):
    me = lax.axis_index(axis)
    other = swap(value, axis, count, across)
    found = [(0, value)] + [(mask, swap(value, axis, count, mask)) for mask in ring]
    found += [(across, other)]
    found += [(across ^ mask, swap(other, axis, count, mask)) for mask in ring]
    whole = jnp.zeros((len(found),) + value.shape, value.dtype)
    for mask, shard in found:
        whole = lax.dynamic_update_index_in_dim(whole, shard, (me ^ mask) >> shift, 0)
    return whole


def on_device(rows, cols, operator, sketch_right, sketch_left):
    core_index = lax.axis_index("row") & 1
    own = gather_grid(sketch_right, "row", rows, ROW_RING, ROW_Z, 1)
    partner = swap(own, "row", rows, CORE)
    first = core_index == 0
    right_rows = jnp.stack(
        [jnp.where(first, own, partner), jnp.where(first, partner, own)], 1
    ).reshape(-1, sketch_right.shape[1])
    left_rows = gather_grid(sketch_left, "col", cols, COL_RING, COL_Z, 0)
    left_rows = left_rows.reshape(-1, sketch_left.shape[1])

    image_term = jnp.dot(operator, right_rows, preferred_element_type=jnp.float32)
    core_term = sum(
        lax.dot_general(left_rows, part, TRANSPOSED, preferred_element_type=jnp.float32)
        for part in three_parts(image_term)
    )
    image_piece = lax.all_to_all(
        image_term.reshape(cols, -1, image_term.shape[1]), "col", 0, 0
    ).sum(0)

    core_term, late_rows = lax.optimization_barrier((core_term, left_rows))
    wide_term = lax.dot_general(
        operator, late_rows, TRANSPOSED, preferred_element_type=jnp.float32
    )
    core = sum_everywhere(core_term, rows * cols)

    halves = wide_term.reshape(rows // 2, 2, -1, wide_term.shape[1])
    mine = lax.dynamic_index_in_dim(halves, core_index, 1, False)
    theirs = lax.dynamic_index_in_dim(halves, 1 - core_index, 1, False)
    paired = mine + swap(theirs, "row", rows, CORE)
    same_core = [[i for i in range(rows) if i % 2 == c] for c in range(2)]
    wide_piece = lax.all_to_all(paired, "row", 0, 0, axis_index_groups=same_core).sum(0)

    lower_inverse, ortho = factors_of(core)
    factor = math.sqrt(N * L)
    left_piece = (
        factor
        * lax.dot_general(
            image_piece,
            lower_inverse,
            (((1,), (1,)), ((), ())),
            precision=HIGHEST,
            preferred_element_type=jnp.float32,
        )
    ).astype(jnp.bfloat16)
    left_factor = gather_grid(left_piece, "col", cols, COL_RING, COL_Z, 0)
    left_factor = left_factor.reshape(-1, left_piece.shape[1])
    right_factor = jnp.dot(wide_piece, ortho, precision=HIGHEST).astype(jnp.bfloat16)
    return (left_factor, right_factor)


def solution(mesh):
    rows, cols = mesh.shape["row"], mesh.shape["col"]
    in_specs = (P("row", "col"), P(("col", "row"), None), P(("row", "col"), None))
    out_specs = (P("row", None), P(("col", "row"), None))
    return jax.shard_map(
        functools.partial(on_device, rows, cols),
        mesh=mesh,
        in_specs=in_specs,
        out_specs=out_specs,
        check_vma=False,
    )
```

```python
import functools
import math

import jax
import jax.numpy as jnp
from jax import lax
from jax.experimental import pallas as pl
from jax.experimental.pallas import tpu as pltpu
from jax.sharding import PartitionSpec as P

N = 36864
L = 576
BLOCK = 128
PANEL = 16
HIGHEST = lax.Precision.HIGHEST
TRANSPOSED = (((0,), (0,)), ((), ()))
CORE, ROW_RING, ROW_Z = 1, (2, 6, 4), 8
COL_RING, COL_Z = (2, 6, 4), 1


def kernel_parts(value):
    high = value.astype(jnp.bfloat16).astype(jnp.float32)
    rest = value - high
    middle = rest.astype(jnp.bfloat16).astype(jnp.float32)
    low = (rest - middle).astype(jnp.bfloat16).astype(jnp.float32)
    return high, middle, low


def rank_update(value):
    high, middle, low = kernel_parts(value)
    left = jnp.concatenate([high, high, middle, high, low, middle], 0).astype(jnp.bfloat16)
    right = jnp.concatenate([high, middle, high, low, high, middle], 0).astype(jnp.bfloat16)
    return lax.dot_general(left, right, TRANSPOSED, preferred_element_type=jnp.float32)


def block_factor(block_ref):
    size = block_ref.shape[0]
    row = lax.broadcasted_iota(jnp.int32, (PANEL, size), 0)
    lane = lax.broadcasted_iota(jnp.int32, (PANEL, size), 1)
    for start in range(0, size, PANEL):
        end = start + PANEL
        panel = block_ref[start:end, :]
        rows = jnp.where(
            (lane >= start) & (lane < end), (lane - start == row).astype(jnp.float32), panel
        )
        columns = [
            jnp.broadcast_to(panel[:, start + j : start + j + 1], (PANEL, size))
            for j in range(PANEL)
        ]
        pivots = jnp.ones((PANEL, size), jnp.float32)
        for i in range(PANEL):
            pivot = columns[i][i : i + 1, :]
            multiple = jnp.where(row > i, columns[i] * (1.0 / pivot), 0.0)
            pivots = jnp.where(row == i, pivot, pivots)
            for j in range(i + 1, PANEL):
                columns[j] = columns[j] - multiple * columns[j][i : i + 1, :]
            rows = rows - multiple * rows[i : i + 1, :]
        rows = rows * lax.rsqrt(pivots)
        block_ref[start:end, :] = rows
        if end < size:
            below = lax.broadcasted_iota(jnp.int32, (size - end, size), 1)
            rest = jnp.where((below >= start) & (below < end), 0.0, block_ref[end:, :])
            block_ref[end:, :] = rest - rank_update(rows)[end:, :]
    down = lax.broadcasted_iota(jnp.int32, (size, size), 0)
    across = lax.broadcasted_iota(jnp.int32, (size, size), 1)
    return jnp.where(down >= across, block_ref[...], 0.0)


def factor_kernel(core_ref, lower_inverse_ref, ortho_ref, block_ref):
    tall, size = ortho_ref.shape
    core = jnp.concatenate(
        [core_ref[at * tall : (at + 1) * tall, :] for at in range(size // BLOCK)], 1
    )
    work = lower_inverse_ref
    dot = functools.partial(
        lax.dot_general, precision=HIGHEST, preferred_element_type=jnp.float32
    )
    work[...] = dot(core, core, TRANSPOSED)
    starts = range(0, size, BLOCK)
    for low in starts:
        high = low + BLOCK
        block_ref[...] = work[low:high, low:high]
        inverse = block_factor(block_ref)
        strip = dot(inverse, work[low:high, :], (((1,), (0,)), ((), ())))
        strip = jnp.concatenate(
            [inverse if at == low else strip[:, at : at + BLOCK] for at in starts], 1
        )
        if high < size:
            change = dot(strip[:, high:], strip, TRANSPOSED)
            for at in starts:
                old = 0.0 if at == low else work[high:, at : at + BLOCK]
                work[high:, at : at + BLOCK] = old - change[:, at : at + BLOCK]
        for at in starts:
            kept = strip[:, at : at + BLOCK]
            work[low:high, at : at + BLOCK] = kept if at <= low else jnp.zeros_like(kept)
    ortho_ref[...] = dot(core, work[...], (((1,), (1,)), ((), ())))


def factors_of(core, tall, size):
    return pl.pallas_call(
        factor_kernel,
        out_shape=[
            jax.ShapeDtypeStruct((size, size), jnp.float32),
            jax.ShapeDtypeStruct((tall, size), jnp.float32),
        ],
        scratch_shapes=[pltpu.VMEM((BLOCK, BLOCK), jnp.float32)],
        compiler_params=pltpu.CompilerParams(vmem_limit_bytes=32 * 2**20),
        cost_estimate=pl.CostEstimate(
            flops=20 * 10**9, bytes_accessed=3 * 10**6, transcendentals=0
        ),
    )(core)


def swap(value, axis, count, mask):
    return lax.ppermute(value, axis, [(i, i ^ mask) for i in range(count)])


def image_kernel(place_ref, operator_ref, own_ref, other_ref, *refs):
    image_ref, upper_refs, near_ref, far_ref, right_ref = refs[0], refs[1:5], *refs[5:]

    @pl.when(pl.program_id(0) == 0)
    def _():
        core_place = place_ref[0] & 1
        shard = own_ref.shape[1]
        for k in range(own_ref.shape[0]):
            for ref, place in ((own_ref, core_place), (other_ref, 1 - core_place)):
                start = pl.multiple_of((2 * k + place) * shard, shard)
                right_ref[pl.ds(start, shard), :] = ref[k]

    image = jnp.dot(operator_ref[...], right_ref[...], preferred_element_type=jnp.float32)
    half = image.shape[0] // 2
    first = (place_ref[1] & 1) == 0
    near = jnp.where(first, image[:half], image[half:])
    far = jnp.where(first, image[half:], image[:half])
    image_ref[0], image_ref[1] = near, far
    near_ref[0], far_ref[0] = near[half // 2 :], far[half // 2 :]
    for k, ref in enumerate(upper_refs):

        @pl.when(pl.program_id(0) == k)
        def _(ref=ref):
            ref[0], ref[1] = near[: half // 2], far[: half // 2]


def image_term(places, operator, own, other):
    height, width = operator.shape
    shard, size = own.shape[1:]
    tile, part = 2 * shard, shard // 2
    shards = pl.BlockSpec(own.shape, lambda i, place: (0, 0, 0))
    grid_spec = pltpu.PrefetchScalarGridSpec(
        num_scalar_prefetch=1,
        grid=(height // tile,),
        in_specs=[
            pl.BlockSpec((tile, width), lambda i, place: ((place[1] >> 1) ^ i, 0)),
            shards,
            shards,
        ],
        out_specs=[pl.BlockSpec((2, shard, size), lambda i, place: (i, 0, 0))]
        + [pl.BlockSpec((2, part, size), lambda i, place: (0, 0, 0))] * 4
        + [pl.BlockSpec((1, part, size), lambda i, place: (i, 0, 0))] * 2,
        scratch_shapes=[pltpu.VMEM((width, size), jnp.bfloat16)],
    )
    return pl.pallas_call(
        image_kernel,
        grid_spec=grid_spec,
        out_shape=[
            jax.ShapeDtypeStruct(shape, jnp.float32)
            for shape in [(height // shard, shard, size)]
            + [(2, part, size)] * 4
            + [(height // tile, part, size)] * 2
        ],
        compiler_params=pltpu.CompilerParams(vmem_limit_bytes=56 * 2**20),
        cost_estimate=pl.CostEstimate(
            flops=12 * 10**9, bytes_accessed=30 * 10**6, transcendentals=0
        ),
    )(places, operator, own, other)


def core_kernel(place_ref, image_ref, *refs):
    left_refs = refs[:8]
    core_ref, left_out_ref, total_ref = refs[8:]
    step = pl.program_id(0)
    shard = image_ref.shape[1]
    starts = [pl.multiple_of((place_ref[1] ^ mask) * shard, shard) for mask in range(8)]

    @pl.when(step == 0)
    def _():
        for start, ref in zip(starts, left_refs):
            left_out_ref[pl.ds(start, shard), :] = ref[...]
        total_ref[...] = jnp.zeros_like(total_ref)

    parts, lefts = [], []
    for k in range(2):
        start = pl.multiple_of((place_ref[1] ^ (2 * step + k)) * shard, shard)
        left = left_out_ref[pl.ds(start, shard), :]
        lefts.append(left)
        parts.append(jnp.concatenate(kernel_parts(image_ref[k]), 1).astype(jnp.bfloat16))
    sums = lax.dot_general(
        jnp.concatenate(lefts, 0),
        jnp.concatenate(parts, 0),
        TRANSPOSED,
        preferred_element_type=jnp.float32,
    )
    size = total_ref.shape[1]
    total_ref[...] += sums[:, :size] + (sums[:, size : 2 * size] + sums[:, 2 * size :])

    @pl.when(step == pl.num_programs(0) - 1)
    def _():
        tall, size = total_ref.shape
        for at in range(size // BLOCK):
            core_ref[at * tall : (at + 1) * tall, :] = total_ref[
                :, at * BLOCK : (at + 1) * BLOCK
            ]
        used = tall * size // BLOCK
        core_ref[used:, :] = jnp.zeros((core_ref.shape[0] - used, BLOCK), jnp.float32)


def core_of(places, image, left_shards, shares):
    count, shard, size = image.shape
    tall = left_shards[0].shape[1]
    grid_spec = pltpu.PrefetchScalarGridSpec(
        num_scalar_prefetch=1,
        grid=(count // 2,),
        in_specs=[pl.BlockSpec((2, shard, size), lambda i, place: (i, 0, 0))]
        + [pl.BlockSpec((shard, tall), lambda i, place: (0, 0))] * count,
        out_specs=[
            pl.BlockSpec((shares * 16, BLOCK), lambda i, place: (0, 0)),
            pl.BlockSpec((count * shard, tall), lambda i, place: (0, 0)),
        ],
        scratch_shapes=[pltpu.VMEM((tall, size), jnp.float32)],
    )
    return pl.pallas_call(
        core_kernel,
        grid_spec=grid_spec,
        out_shape=[
            jax.ShapeDtypeStruct((shares * 16, BLOCK), jnp.float32),
            jax.ShapeDtypeStruct((count * shard, tall), jnp.bfloat16),
        ],
        compiler_params=pltpu.CompilerParams(vmem_limit_bytes=56 * 2**20),
        cost_estimate=pl.CostEstimate(
            flops=4 * 10**9, bytes_accessed=7 * 10**6, transcendentals=0
        ),
    )(places, image, *left_shards)


def wide_kernel(place_ref, operator_ref, left_ref, *refs):
    outs, left_t_ref = refs[:4], refs[4]
    shard = 2 * outs[0].shape[1]
    core_place, y_low = place_ref[0] & 1, (place_ref[0] >> 1) & 1

    @pl.when(pl.program_id(0) == 0)
    def _():
        left_t_ref[...] = left_ref[...].T

    wide = jnp.dot(left_t_ref[...], operator_ref[...], preferred_element_type=jnp.float32).T
    pieces = [wide[k * shard : (k + 1) * shard, :] for k in range(4)]
    first_core, first_y = core_place == 0, y_low == 0
    for which in range(2):
        of_core = [
            jnp.where(first_core, pieces[2 * y + which], pieces[2 * y + 1 - which])
            for y in range(2)
        ]
        for slot in range(2):
            piece = jnp.where(first_y, of_core[slot], of_core[1 - slot])
            outs[2 * which][slot] = piece[: shard // 2, :]
            outs[2 * which + 1][slot] = piece[shard // 2 :, :]


def wide_terms(places, operator, left_rows, shard):
    height, width = operator.shape
    tall = left_rows.shape[1]
    steps, half = width // (4 * shard), shard // 2
    grid_spec = pltpu.PrefetchScalarGridSpec(
        num_scalar_prefetch=1,
        grid=(steps,),
        in_specs=[
            pl.BlockSpec((height, 4 * shard), lambda j, place: (0, (place[0] >> 2) ^ j)),
            pl.BlockSpec((height, tall), lambda j, place: (0, 0)),
        ],
        out_specs=[pl.BlockSpec((2, half, tall), lambda j, place: (j, 0, 0))] * 4,
        scratch_shapes=[pltpu.VMEM((tall, height), jnp.bfloat16)],
    )
    return pl.pallas_call(
        wide_kernel,
        grid_spec=grid_spec,
        out_shape=[jax.ShapeDtypeStruct((2 * steps, half, tall), jnp.float32)] * 4,
        compiler_params=pltpu.CompilerParams(vmem_limit_bytes=56 * 2**20),
        cost_estimate=pl.CostEstimate(
            flops=13 * 10**9, bytes_accessed=35 * 10**6, transcendentals=0
        ),
    )(places, operator, left_rows)


def sum_shares(value, count):
    return lax.all_to_all(value.reshape(count, -1, BLOCK), ("row", "col"), 0, 0).sum(0)


def gather_shares(share, count):
    copies = jnp.broadcast_to(share[None], (count,) + share.shape)
    return lax.all_to_all(copies, ("row", "col"), 0, 0).reshape(-1, share.shape[-1])


def scatter_first(upper, lower, far, axis, count, ring, across):
    sends = [swap(pair, axis, count, mask) for pair, mask in zip(upper[1:], ring)]
    return upper[0], sends, lower, swap(far, axis, count, across)


def scatter_last(state, axis, count, ring, across):
    own, sends, lower, crossed = state
    upper_far = own[1] + sum(send[1] for send in sends)
    upper_sum = own[0] + sum(send[0] for send in sends)
    upper_sum = upper_sum + swap(upper_far, axis, count, across)
    lower_sum = lower[0] + crossed[0]
    for k in range(1, 4):
        at = ring[k - 1] >> 1 if axis == "col" else k
        lower_sum = lower_sum + swap(lower[k] + crossed[at], axis, count, ring[k - 1])
    return jnp.concatenate([upper_sum, lower_sum], 0)


def on_device(rows, cols, operator, sketch_right, sketch_left):
    places = jnp.stack([lax.axis_index("row"), lax.axis_index("col")]).astype(jnp.int32)
    shard = sketch_right.shape[0]
    join = lax.optimization_barrier
    row_axis = ("row", rows, ROW_RING, ROW_Z)
    col_axis = ("col", cols, COL_RING, COL_Z)

    left_far = swap(sketch_left, "col", cols, COL_Z)
    left_near = [swap(sketch_left, "col", cols, mask) for mask in COL_RING]
    same_core = [[i for i in range(rows) if i % 2 == c] for c in range(2)]
    own = lax.all_to_all(
        jnp.broadcast_to(sketch_right[None], (rows // 2,) + sketch_right.shape),
        "row",
        0,
        0,
        axis_index_groups=same_core,
    )
    own, left_far, left_near = join((own, left_far, left_near))
    left_beyond = [swap(left_far, "col", cols, mask) for mask in COL_RING]
    image, *messages = image_term(places, operator, own, swap(own, "row", rows, CORE))
    image, messages, left_beyond = join((image, messages, left_beyond))
    left_shards = {0: sketch_left, COL_Z: left_far}
    left_shards.update(zip(COL_RING, left_near))
    left_shards.update((COL_Z ^ mask, shard) for mask, shard in zip(COL_RING, left_beyond))
    core_term, left_rows = core_of(
        places, image, [left_shards[mask] for mask in range(cols)], rows * cols
    )

    core_share = sum_shares(core_term, rows * cols)
    upper, near, far = [messages[mask >> 1] for mask in (0, *COL_RING)], *messages[4:]
    image_state = scatter_first(
        upper, [near[mask >> 1] for mask in (0, *COL_RING)], far, *col_axis
    )
    wide_pieces = wide_terms(places, operator, left_rows, shard)
    core_share, wide_pieces = join((core_share, wide_pieces))

    core = gather_shares(core_share, rows * cols)
    mine_upper, mine_lower, other_upper, other_lower = wide_pieces
    other_upper = swap(other_upper, "row", rows, CORE)
    other_lower = swap(other_lower, "row", rows, CORE)
    order = [mask >> 1 for mask in (0, *ROW_RING)]
    upper = [
        jnp.stack([mine_upper[k] + other_upper[k], mine_upper[4 ^ k] + other_upper[4 ^ k]])
        for k in order
    ]
    lower = [mine_lower[k] + other_lower[k] for k in order]
    far = jnp.stack([mine_lower[4 ^ k] + other_lower[4 ^ k] for k in order])
    core, upper, lower, far, image_state = join((core, upper, lower, far, image_state))

    wide_state = scatter_first(upper, lower, far, *row_axis)
    image_piece = scatter_last(image_state, *col_axis)
    tall, size = sketch_left.shape[1], sketch_right.shape[1]
    lower_inverse, ortho = factors_of(core, tall, size)
    wide_state, image_piece, lower_inverse, ortho = join(
        (wide_state, image_piece, lower_inverse, ortho)
    )

    wide_piece = scatter_last(wide_state, *row_axis)
    factor = math.sqrt(N * L)
    left_piece = (
        factor
        * lax.dot_general(
            image_piece,
            lower_inverse,
            (((1,), (1,)), ((), ())),
            precision=HIGHEST,
            preferred_element_type=jnp.float32,
        )
    ).astype(jnp.bfloat16)
    left_factor = lax.all_to_all(
        jnp.broadcast_to(left_piece[None], (cols,) + left_piece.shape), "col", 0, 0
    ).reshape(-1, size)
    right_factor = jnp.dot(wide_piece, ortho, precision=HIGHEST).astype(jnp.bfloat16)
    return (left_factor, right_factor)


def solution(mesh):
    rows, cols = mesh.shape["row"], mesh.shape["col"]
    in_specs = (P("row", "col"), P(("col", "row"), None), P(("row", "col"), None))
    out_specs = (P("row", None), P(("col", "row"), None))
    return jax.shard_map(
        functools.partial(on_device, rows, cols),
        mesh=mesh,
        in_specs=in_specs,
        out_specs=out_specs,
        check_vma=False,
    )
```

```python
import functools
import math

import jax
import jax.numpy as jnp
from jax import lax
from jax.experimental import pallas as pl
from jax.experimental.pallas import tpu as pltpu
from jax.sharding import PartitionSpec as P

N = 36864
L = 576
BLOCK = 128
PANEL = 16
HIGHEST = lax.Precision.HIGHEST
TRANSPOSED = (((0,), (0,)), ((), ()))
CORE, ROW_RING, ROW_Z = 1, (2, 6, 4), 8
COL_RING, COL_Z = (2, 6, 4), 1


def kernel_parts(value):
    high = value.astype(jnp.bfloat16).astype(jnp.float32)
    rest = value - high
    middle = rest.astype(jnp.bfloat16).astype(jnp.float32)
    low = (rest - middle).astype(jnp.bfloat16).astype(jnp.float32)
    return high, middle, low


def rank_update(value):
    high, middle, low = kernel_parts(value)
    left = jnp.concatenate([high, high, middle, high, low, middle], 0).astype(jnp.bfloat16)
    right = jnp.concatenate([high, middle, high, low, high, middle], 0).astype(jnp.bfloat16)
    return lax.dot_general(left, right, TRANSPOSED, preferred_element_type=jnp.float32)


def block_factor(block_ref):
    size = block_ref.shape[0]
    row = lax.broadcasted_iota(jnp.int32, (PANEL, size), 0)
    lane = lax.broadcasted_iota(jnp.int32, (PANEL, size), 1)
    for start in range(0, size, PANEL):
        end = start + PANEL
        panel = block_ref[start:end, :]
        rows = jnp.where(
            (lane >= start) & (lane < end), (lane - start == row).astype(jnp.float32), panel
        )
        columns = [
            jnp.broadcast_to(panel[:, start + j : start + j + 1], (PANEL, size))
            for j in range(PANEL)
        ]
        pivots = jnp.ones((PANEL, size), jnp.float32)
        for i in range(PANEL):
            pivot = columns[i][i : i + 1, :]
            multiple = jnp.where(row > i, columns[i] * (1.0 / pivot), 0.0)
            pivots = jnp.where(row == i, pivot, pivots)
            for j in range(i + 1, PANEL):
                columns[j] = columns[j] - multiple * columns[j][i : i + 1, :]
            rows = rows - multiple * rows[i : i + 1, :]
        rows = rows * lax.rsqrt(pivots)
        block_ref[start:end, :] = rows
        if end < size:
            below = lax.broadcasted_iota(jnp.int32, (size - end, size), 1)
            rest = jnp.where((below >= start) & (below < end), 0.0, block_ref[end:, :])
            block_ref[end:, :] = rest - rank_update(rows)[end:, :]
    down = lax.broadcasted_iota(jnp.int32, (size, size), 0)
    across = lax.broadcasted_iota(jnp.int32, (size, size), 1)
    return jnp.where(down >= across, block_ref[...], 0.0)


def factor_kernel(core_ref, lower_inverse_ref, ortho_ref, block_ref):
    tall, size = ortho_ref.shape
    core = jnp.concatenate(
        [core_ref[at * tall : (at + 1) * tall, :] for at in range(size // BLOCK)], 1
    )
    work = lower_inverse_ref
    dot = functools.partial(
        lax.dot_general, precision=HIGHEST, preferred_element_type=jnp.float32
    )
    work[...] = dot(core, core, TRANSPOSED)
    starts = range(0, size, BLOCK)
    for low in starts:
        high = low + BLOCK
        block_ref[...] = work[low:high, low:high]
        inverse = block_factor(block_ref)
        strip = dot(inverse, work[low:high, :], (((1,), (0,)), ((), ())))
        strip = jnp.concatenate(
            [inverse if at == low else strip[:, at : at + BLOCK] for at in starts], 1
        )
        if high < size:
            change = dot(strip[:, high:], strip, TRANSPOSED)
            for at in starts:
                old = 0.0 if at == low else work[high:, at : at + BLOCK]
                work[high:, at : at + BLOCK] = old - change[:, at : at + BLOCK]
        for at in starts:
            kept = strip[:, at : at + BLOCK]
            work[low:high, at : at + BLOCK] = kept if at <= low else jnp.zeros_like(kept)
    ortho_ref[...] = dot(core, work[...], (((1,), (1,)), ((), ())))


def factors_of(core, tall, size):
    return pl.pallas_call(
        factor_kernel,
        out_shape=[
            jax.ShapeDtypeStruct((size, size), jnp.float32),
            jax.ShapeDtypeStruct((tall, size), jnp.float32),
        ],
        scratch_shapes=[pltpu.VMEM((BLOCK, BLOCK), jnp.float32)],
        compiler_params=pltpu.CompilerParams(vmem_limit_bytes=32 * 2**20),
        cost_estimate=pl.CostEstimate(
            flops=20 * 10**9, bytes_accessed=3 * 10**6, transcendentals=0
        ),
    )(core)


def swap(value, axis, count, mask):
    return lax.ppermute(value, axis, [(i, i ^ mask) for i in range(count)])


def image_kernel(place_ref, operator_ref, own_ref, other_ref, *refs):
    image_ref, upper_refs, near_ref, far_ref, right_ref = refs[0], refs[1:5], *refs[5:]

    @pl.when(pl.program_id(0) == 0)
    def _():
        core_place = place_ref[0] & 1
        shard = own_ref.shape[1]
        for k in range(own_ref.shape[0]):
            for ref, place in ((own_ref, core_place), (other_ref, 1 - core_place)):
                start = pl.multiple_of((2 * k + place) * shard, shard)
                right_ref[pl.ds(start, shard), :] = ref[k]

    image = jnp.dot(operator_ref[...], right_ref[...], preferred_element_type=jnp.float32)
    half = image.shape[0] // 2
    first = (place_ref[1] & 1) == 0
    near = jnp.where(first, image[:half], image[half:])
    far = jnp.where(first, image[half:], image[:half])
    image_ref[0], image_ref[1] = near, far
    near_ref[0], far_ref[0] = near[half // 2 :], far[half // 2 :]
    for k, ref in enumerate(upper_refs):

        @pl.when(pl.program_id(0) == k)
        def _(ref=ref):
            ref[0], ref[1] = near[: half // 2], far[: half // 2]


def image_term(places, operator, own, other):
    height, width = operator.shape
    shard, size = own.shape[1:]
    tile, part = 2 * shard, shard // 2
    shards = pl.BlockSpec(own.shape, lambda i, place: (0, 0, 0))
    grid_spec = pltpu.PrefetchScalarGridSpec(
        num_scalar_prefetch=1,
        grid=(height // tile,),
        in_specs=[
            pl.BlockSpec((tile, width), lambda i, place: ((place[1] >> 1) ^ i, 0)),
            shards,
            shards,
        ],
        out_specs=[pl.BlockSpec((2, shard, size), lambda i, place: (i, 0, 0))]
        + [pl.BlockSpec((2, part, size), lambda i, place: (0, 0, 0))] * 4
        + [pl.BlockSpec((1, part, size), lambda i, place: (i, 0, 0))] * 2,
        scratch_shapes=[pltpu.VMEM((width, size), jnp.bfloat16)],
    )
    return pl.pallas_call(
        image_kernel,
        grid_spec=grid_spec,
        out_shape=[
            jax.ShapeDtypeStruct(shape, jnp.float32)
            for shape in [(height // shard, shard, size)]
            + [(2, part, size)] * 4
            + [(height // tile, part, size)] * 2
        ],
        compiler_params=pltpu.CompilerParams(vmem_limit_bytes=56 * 2**20),
        cost_estimate=pl.CostEstimate(
            flops=12 * 10**9, bytes_accessed=30 * 10**6, transcendentals=0
        ),
    )(places, operator, own, other)


def core_kernel(place_ref, image_ref, *refs):
    left_refs = refs[:8]
    core_ref, left_out_ref, total_ref = refs[8:]
    step = pl.program_id(0)
    shard = image_ref.shape[1]
    starts = [pl.multiple_of((place_ref[1] ^ mask) * shard, shard) for mask in range(8)]

    @pl.when(step == 0)
    def _():
        for start, ref in zip(starts, left_refs):
            left_out_ref[pl.ds(start, shard), :] = ref[...]
        total_ref[...] = jnp.zeros_like(total_ref)

    parts, lefts = [], []
    for k in range(2):
        start = pl.multiple_of((place_ref[1] ^ (2 * step + k)) * shard, shard)
        left = left_out_ref[pl.ds(start, shard), :]
        lefts.append(left)
        parts.append(jnp.concatenate(kernel_parts(image_ref[k]), 1).astype(jnp.bfloat16))
    sums = lax.dot_general(
        jnp.concatenate(lefts, 0),
        jnp.concatenate(parts, 0),
        TRANSPOSED,
        preferred_element_type=jnp.float32,
    )
    size = total_ref.shape[1]
    total_ref[...] += sums[:, :size] + (sums[:, size : 2 * size] + sums[:, 2 * size :])

    @pl.when(step == pl.num_programs(0) - 1)
    def _():
        tall, size = total_ref.shape
        for at in range(size // BLOCK):
            core_ref[at * tall : (at + 1) * tall, :] = total_ref[
                :, at * BLOCK : (at + 1) * BLOCK
            ]
        used = tall * size // BLOCK
        core_ref[used:, :] = jnp.zeros((core_ref.shape[0] - used, BLOCK), jnp.float32)


def core_of(places, image, left_shards, shares):
    count, shard, size = image.shape
    tall = left_shards[0].shape[1]
    grid_spec = pltpu.PrefetchScalarGridSpec(
        num_scalar_prefetch=1,
        grid=(count // 2,),
        in_specs=[pl.BlockSpec((2, shard, size), lambda i, place: (i, 0, 0))]
        + [pl.BlockSpec((shard, tall), lambda i, place: (0, 0))] * count,
        out_specs=[
            pl.BlockSpec((shares * 16, BLOCK), lambda i, place: (0, 0)),
            pl.BlockSpec((count * shard, tall), lambda i, place: (0, 0)),
        ],
        scratch_shapes=[pltpu.VMEM((tall, size), jnp.float32)],
    )
    return pl.pallas_call(
        core_kernel,
        grid_spec=grid_spec,
        out_shape=[
            jax.ShapeDtypeStruct((shares * 16, BLOCK), jnp.float32),
            jax.ShapeDtypeStruct((count * shard, tall), jnp.bfloat16),
        ],
        compiler_params=pltpu.CompilerParams(vmem_limit_bytes=56 * 2**20),
        cost_estimate=pl.CostEstimate(
            flops=4 * 10**9, bytes_accessed=7 * 10**6, transcendentals=0
        ),
    )(places, image, *left_shards)


def wide_kernel(place_ref, operator_ref, left_ref, *refs):
    outs, left_t_ref = refs[:4], refs[4]
    shard = 2 * outs[0].shape[1]
    core_place, y_low = place_ref[0] & 1, (place_ref[0] >> 1) & 1

    @pl.when(pl.program_id(0) == 0)
    def _():
        left_t_ref[...] = left_ref[...].T

    wide = jnp.dot(left_t_ref[...], operator_ref[...], preferred_element_type=jnp.float32).T
    pieces = [wide[k * shard : (k + 1) * shard, :] for k in range(4)]
    first_core, first_y = core_place == 0, y_low == 0
    for which in range(2):
        of_core = [
            jnp.where(first_core, pieces[2 * y + which], pieces[2 * y + 1 - which])
            for y in range(2)
        ]
        for slot in range(2):
            piece = jnp.where(first_y, of_core[slot], of_core[1 - slot])
            outs[2 * which][slot] = piece[: shard // 2, :]
            outs[2 * which + 1][slot] = piece[shard // 2 :, :]


def wide_terms(places, operator, left_rows, shard):
    height, width = operator.shape
    tall = left_rows.shape[1]
    steps, half = width // (4 * shard), shard // 2
    grid_spec = pltpu.PrefetchScalarGridSpec(
        num_scalar_prefetch=1,
        grid=(steps,),
        in_specs=[
            pl.BlockSpec((height, 4 * shard), lambda j, place: (0, (place[0] >> 2) ^ j)),
            pl.BlockSpec((height, tall), lambda j, place: (0, 0)),
        ],
        out_specs=[pl.BlockSpec((2, half, tall), lambda j, place: (j, 0, 0))] * 4,
        scratch_shapes=[pltpu.VMEM((tall, height), jnp.bfloat16)],
    )
    return pl.pallas_call(
        wide_kernel,
        grid_spec=grid_spec,
        out_shape=[jax.ShapeDtypeStruct((2 * steps, half, tall), jnp.float32)] * 4,
        compiler_params=pltpu.CompilerParams(vmem_limit_bytes=56 * 2**20),
        cost_estimate=pl.CostEstimate(
            flops=13 * 10**9, bytes_accessed=35 * 10**6, transcendentals=0
        ),
    )(places, operator, left_rows)


def sum_shares(value, count):
    return lax.all_to_all(value.reshape(count, -1, BLOCK), ("row", "col"), 0, 0).sum(0)


def gather_shares(share, count):
    copies = jnp.broadcast_to(share[None], (count,) + share.shape)
    return lax.all_to_all(copies, ("row", "col"), 0, 0).reshape(-1, share.shape[-1])


def scatter_first(upper, lower, far, axis, count, ring, across):
    sends = [swap(pair, axis, count, mask) for pair, mask in zip(upper[1:], ring)]
    return upper[0], sends, lower, swap(far, axis, count, across)


def scatter_last(state, axis, count, ring, across):
    own, sends, lower, crossed = state
    upper_far = own[1] + sum(send[1] for send in sends)
    upper_sum = own[0] + sum(send[0] for send in sends)
    upper_sum = upper_sum + swap(upper_far, axis, count, across)
    lower_sum = lower[0] + crossed[0]
    for k in range(1, 4):
        at = ring[k - 1] >> 1 if axis == "col" else k
        lower_sum = lower_sum + swap(lower[k] + crossed[at], axis, count, ring[k - 1])
    return jnp.concatenate([upper_sum, lower_sum], 0)


def on_device(rows, cols, operator, sketch_right, sketch_left):
    places = jnp.stack([lax.axis_index("row"), lax.axis_index("col")]).astype(jnp.int32)
    shard = sketch_right.shape[0]
    join = lax.optimization_barrier
    row_axis = ("row", rows, ROW_RING, ROW_Z)
    col_axis = ("col", cols, COL_RING, COL_Z)

    left_far = swap(sketch_left, "col", cols, COL_Z)
    left_near = [swap(sketch_left, "col", cols, mask) for mask in COL_RING]
    same_core = [[i for i in range(rows) if i % 2 == c] for c in range(2)]
    own = lax.all_to_all(
        jnp.broadcast_to(sketch_right[None], (rows // 2,) + sketch_right.shape),
        "row",
        0,
        0,
        axis_index_groups=same_core,
    )
    own, left_far, left_near = join((own, left_far, left_near))
    left_beyond = [swap(left_far, "col", cols, mask) for mask in COL_RING]
    image, *messages = image_term(places, operator, own, swap(own, "row", rows, CORE))
    image, messages, left_beyond = join((image, messages, left_beyond))
    left_shards = {0: sketch_left, COL_Z: left_far}
    left_shards.update(zip(COL_RING, left_near))
    left_shards.update((COL_Z ^ mask, shard) for mask, shard in zip(COL_RING, left_beyond))
    core_term, left_rows = core_of(
        places, image, [left_shards[mask] for mask in range(cols)], rows * cols
    )

    core_share = sum_shares(core_term, rows * cols)
    upper, near, far = [messages[mask >> 1] for mask in (0, *COL_RING)], *messages[4:]
    image_state = scatter_first(
        upper, [near[mask >> 1] for mask in (0, *COL_RING)], far, *col_axis
    )
    wide_pieces = wide_terms(places, operator, left_rows, shard)
    core_share, wide_pieces, image_state = join((core_share, wide_pieces, image_state))

    core = gather_shares(core_share, rows * cols)
    mine_upper, mine_lower, other_upper, other_lower = wide_pieces
    other_upper = swap(other_upper, "row", rows, CORE)
    other_lower = swap(other_lower, "row", rows, CORE)
    order = [mask >> 1 for mask in (0, *ROW_RING)]
    upper = [
        jnp.stack([mine_upper[k] + other_upper[k], mine_upper[4 ^ k] + other_upper[4 ^ k]])
        for k in order
    ]
    lower = [mine_lower[k] + other_lower[k] for k in order]
    far = jnp.stack([mine_lower[4 ^ k] + other_lower[4 ^ k] for k in order])
    core, upper, lower, far, image_state = join((core, upper, lower, far, image_state))

    wide_state = scatter_first(upper, lower, far, *row_axis)
    image_piece = scatter_last(image_state, *col_axis)
    tall, size = sketch_left.shape[1], sketch_right.shape[1]
    lower_inverse, ortho = factors_of(core, tall, size)
    wide_state, image_piece, lower_inverse, ortho = join(
        (wide_state, image_piece, lower_inverse, ortho)
    )

    wide_piece = scatter_last(wide_state, *row_axis)
    factor = math.sqrt(N * L)
    left_piece = (
        factor
        * lax.dot_general(
            image_piece,
            lower_inverse,
            (((1,), (1,)), ((), ())),
            precision=HIGHEST,
            preferred_element_type=jnp.float32,
        )
    ).astype(jnp.bfloat16)
    left_factor = lax.all_to_all(
        jnp.broadcast_to(left_piece[None], (cols,) + left_piece.shape), "col", 0, 0
    ).reshape(-1, size)
    right_factor = jnp.dot(wide_piece, ortho, precision=HIGHEST).astype(jnp.bfloat16)
    return (left_factor, right_factor)


def solution(mesh):
    rows, cols = mesh.shape["row"], mesh.shape["col"]
    in_specs = (P("row", "col"), P(("col", "row"), None), P(("row", "col"), None))
    out_specs = (P("row", None), P(("col", "row"), None))
    return jax.shard_map(
        functools.partial(on_device, rows, cols),
        mesh=mesh,
        in_specs=in_specs,
        out_specs=out_specs,
        check_vma=False,
    )
```
